512 devices in a mesh: row: 32 (over x_hi, z), col: 16 (over x_lo, y, core).
Axes of the slice: x: 4 (x_hi: 2, x_lo: 2; x = x_hi * 2 + x_lo), y: 4, z: 16, core: 2. Of those that a mesh axis runs over, the one named last changes fastest.
Arguments:
- tokens: bfloat16 [512, 8192], P('row'), may hold values from -48 to 48
- weight: bfloat16 [8192, 14336], P('col', 'row'), may hold values from -0.0625 to 0.0625
- grad_in: bfloat16 [512, 14336], P('col', 'row'), may hold values from -48 to 48
Outputs:
- act_cov: float32 [8192, 8192], P('row', 'col')
- grad_cov: float32 [14336, 14336], P('row', 'col')
The draws below stay inside these ranges and needn't reach their ends.
All inputs are finite; a program needn't handle non-finite values.
Results may differ from the reference program's by a relative error of at most 0.004.
Values may be sent and summed in bfloat16 or wider, within the bound.
No kernel may reach another device: no remote copies, remote signals or barrier semaphores. Data moves between devices by JAX's collectives and lax.ppermute only.
A program may use at most 64 MiB of HBM per device.

```python
import math
import jax
import jax.numpy as jnp
from jax import lax

D = 8192
HID = 14336
TOKENS = 512


def scaled_field(base, key, row_count, col_count):
    row_key, col_key = jax.random.split(key)
    row_scale = jnp.exp(jax.random.uniform(row_key, (row_count, 1), minval=math.log(0.3), maxval=math.log(3.0)))
    col_scale = jnp.exp(jax.random.uniform(col_key, (1, col_count), minval=math.log(0.5), maxval=math.log(2.0)))
    return base * row_scale * col_scale


def draw_tokens(key, part):
    key = jax.random.fold_in(key, 11)
    base_key = jax.random.fold_in(key, 0)
    scale_key = jax.random.fold_in(key, 2)
    base = jnp.clip(jax.random.normal(base_key, (TOKENS, D)), -7.5, 7.5)
    return scaled_field(base, scale_key, TOKENS, D).astype(jnp.bfloat16)


def draw_grad_in(key, part):
    key = jax.random.fold_in(key, 23)
    base_key = jax.random.fold_in(key, 0)
    scale_key = jax.random.fold_in(key, 2)
    base = jnp.clip(jax.random.normal(base_key, (TOKENS, HID)), -7.5, 7.5)
    return scaled_field(base, scale_key, TOKENS, HID).astype(jnp.bfloat16)


def level_of(key, dims, cuts, least, largest):
    gain, own = 1.0, jax.random.fold_in(key, 6)
    for axis_at, blocks in cuts:
        draws = jnp.exp(jax.random.uniform(jax.random.fold_in(own, axis_at), (blocks,), jnp.float32, least / len(cuts), largest / len(cuts)))
        gain = gain * jnp.repeat(draws, dims[axis_at] // blocks).reshape([-1 if axis == axis_at else 1 for axis in range(len(dims))])
    return gain


def bell_draw(own_key, shape, deviation, bound, cuts=(), held_as=jnp.bfloat16):
    gain = level_of(own_key, shape, cuts, -0.22, 0.18) if cuts else 1.0
    drawn = jax.random.normal(own_key, shape, jnp.float32) * deviation * gain
    return jnp.minimum(jnp.maximum(drawn, -bound), bound).astype(held_as)


def setup_inputs(seed: int = 0) -> dict:
    key_list = jax.random.split(jax.random.key(seed), 4)
    return {
        "tokens": draw_tokens(jax.random.fold_in(key_list[3], 71), 0),
        "weight": bell_draw(key_list[1], (D, HID), D ** -0.5, 0.0625, ((0, 16), (1, 32))),
        "grad_in": draw_grad_in(jax.random.fold_in(key_list[3], 71), 0),
    }


def silu_slope(pre_act):
    sigmoid_value = jax.nn.sigmoid(pre_act)
    return sigmoid_value * (1.0 + pre_act * (1.0 - sigmoid_value))


def reference(tokens, weight, grad_in):
    token_count = tokens.shape[0]
    pre_act = jnp.dot(tokens, weight, preferred_element_type=jnp.float32)
    slope_grad = (grad_in.astype(jnp.float32) * silu_slope(pre_act)).astype(jnp.bfloat16)
    contract = (((0,), (0,)), ((), ()))
    act_cov = lax.dot_general(tokens, tokens, contract, preferred_element_type=jnp.float32) / token_count
    grad_cov = lax.dot_general(slope_grad, slope_grad, contract, preferred_element_type=jnp.float32) / token_count
    return act_cov, grad_cov
```

```python
import jax
import jax.numpy as jnp
from jax import lax
from jax.sharding import Mesh, PartitionSpec as P

ROW = ("xh", "z")
COL = ("xl", "y", "core")
LEVEL = ("xh", "xl", "y", "core")
SIZES = (2, 16, 2, 4, 2)
CONTRACT = (((0,), (0,)), ((), ()))
LANES = 512


def exchange(parts, axis):
    return lax.all_to_all(parts, axis, split_axis=0, concat_axis=0, tiled=True)


def silu_slope(pre_act):
    sigmoid_value = jax.nn.sigmoid(pre_act)
    return sigmoid_value * (1.0 + pre_act * (1.0 - sigmoid_value))


def dot(a, b):
    return lax.dot_general(a, b, CONTRACT, preferred_element_type=jnp.float32)


def shards(tokens, weight, grad_in):
    tok, feats = tokens.shape
    hid = weight.shape[1]
    fcol = weight.shape[0]
    nx, nz, _, ny, nc = SIZES
    ncol = 2 * ny * nc
    rfeat = feats // (nx * nz)
    xh, xl, z = (lax.axis_index(a) for a in ("xh", "xl", "z"))
    col = lax.axis_index(COL)
    token_count = tok * nx * nz

    own_cols = lax.dynamic_slice_in_dim(tokens, col * fcol, fcol, 1)
    half = exchange(jnp.broadcast_to(own_cols[None], (nz, tok, fcol)), "z")
    half = half.reshape(nz * tok, fcol)
    swap = [(0, 1), (1, 0)]
    other_weight = lax.ppermute(weight, "xh", swap)
    pair0 = jnp.where(xh == 0, weight, other_weight)
    pair1 = jnp.where(xh == 0, other_weight, weight)

    halves = grad_in.reshape(2, tok, hid)
    squares = [(0, 0), (0, 1), (1, 0), (1, 1)]
    from_a = lax.ppermute(
        jnp.where(xh == 0, halves[0], halves[1]), ("xh", "xl"), [(2 * a + b, 2 * b + a) for a, b in squares]
    )
    from_b = lax.ppermute(
        jnp.where(xh == 0, halves[1], halves[0]), ("xh", "xl"), [(2 * a + b, 2 * b + 1 - a) for a, b in squares]
    )
    cot = jnp.stack([jnp.where(xl == 0, from_a, from_b), jnp.where(xl == 0, from_b, from_a)])

    part = jnp.stack([jnp.dot(half, w, preferred_element_type=jnp.float32) for w in (pair0, pair1)])
    part = part.reshape(nx, ny * nc, 2, tok, hid).transpose(2, 1, 0, 3, 4)
    part = part.reshape(ncol, nx, tok, hid)
    pre_act = jnp.sum(exchange(part, COL), axis=0)
    slope = (cot.astype(jnp.float32) * silu_slope(pre_act)).astype(jnp.bfloat16)
    slope = jnp.pad(slope, ((0, 0), (0, 0), (0, LANES - hid)))

    own_token = lax.dynamic_slice_in_dim(tokens, col, 1, 0).reshape(1, tok, LANES)
    lines = lax.all_gather(jnp.concatenate([slope, own_token], axis=0), "z", axis=0, tiled=False)
    panels = lines[:, :2].reshape(ny * nc, 2, nx, tok, LANES).transpose(2, 0, 1, 3, 4)
    panels = jnp.broadcast_to(panels.reshape(1, ncol, 2 * tok, LANES), (nx, ncol, 2 * tok, LANES))
    rows = jnp.broadcast_to(slope[:, None], (nx, ncol, tok, LANES))
    picked = lines[:, 2].reshape(2, nz // 2, nx, nz // 2, 2, rfeat)
    picked = lax.dynamic_index_in_dim(picked, z // 2, 3, keepdims=False)
    picked = jnp.where(z % 2 == 0, picked[:, :, :, 0], picked[:, :, :, 1])
    picked = picked.transpose(2, 1, 0, 3).reshape(nx, 1, nz // 2, LANES)
    picked = jnp.broadcast_to(picked, (nx, ncol, nz // 2, LANES))
    pieces = jnp.concatenate([rows, panels, picked], axis=2).reshape(nx * ncol, -1, LANES)
    pieces = exchange(pieces, LEVEL)

    row_block = pieces[:, :tok, :hid].reshape(-1, hid)
    tiles = [
        dot(row_block, pieces[:, (1 + b) * tok : (2 + b) * tok, :hid].reshape(-1, hid)) for b in range(2)
    ]
    grad_cov = jnp.concatenate(tiles, axis=1) / token_count

    other_half = lax.ppermute(half, "xh", swap)
    cols = jnp.stack([jnp.where(xh == 0, half, other_half), jnp.where(xh == 0, other_half, half)])
    cols = cols.reshape(nx, 2, nz // 2, tok, fcol).transpose(1, 0, 3, 2, 4).reshape(2, -1, fcol)
    act_rows = pieces[:, 3 * tok :].reshape(-1, LANES)
    act_cov = (dot(act_rows[:, :rfeat], cols[0]) + dot(act_rows[:, rfeat:], cols[1])) / token_count
    return act_cov, grad_cov


def solution(mesh):
    fine = Mesh(mesh.devices.reshape(SIZES), ("xh", "z", "xl", "y", "core"))
    placed = (P(ROW, None), P(COL, ROW), P(COL, ROW))
    return jax.shard_map(
        shards,
        mesh=fine,
        in_specs=placed,
        out_specs=(P(ROW, COL), P(ROW, COL)),
        check_vma=False,
    )
```

```python
import jax
import jax.numpy as jnp
from jax import lax
from jax.sharding import Mesh, PartitionSpec as P

ROW = ("xh", "z")
COL = ("xl", "y", "core")
LEVEL = ("xh", "xl", "y", "core")
SIZES = (2, 16, 2, 4, 2)
CONTRACT = (((0,), (0,)), ((), ()))
LANES = 512


def exchange(parts, axis):
    return lax.all_to_all(parts, axis, split_axis=0, concat_axis=0, tiled=True)


def silu_slope(pre_act):
    sigmoid_value = jax.nn.sigmoid(pre_act)
    return sigmoid_value * (1.0 + pre_act * (1.0 - sigmoid_value))


def dot(a, b):
    return lax.dot_general(a, b, CONTRACT, preferred_element_type=jnp.float32)


def to_tiles(x):
    lead, (rows, lanes) = x.shape[:-2], x.shape[-2:]
    x = x.reshape(*lead, rows // 8, 8, lanes // 128, 128)
    return jnp.swapaxes(x, -3, -2).reshape(*lead, -1, 8, 128)


def from_tiles(x, rows):
    lead = x.shape[:-3]
    x = x.reshape(*lead, rows // 8, -1, 8, 128)
    return jnp.swapaxes(x, -3, -2).reshape(*lead, rows, -1)


def moves(source_bit):
    pairs = []
    for xh in range(2):
        for xl in range(2):
            for k in range(8):
                source = (xh * 2 + xl) * 8 + k
                core = xh if source_bit == 0 else 1 - xh
                pairs.append((source, ((xl * 2 + k // 4) * 4 + k % 4) * 2 + core))
    return pairs


def shards(tokens, weight, grad_in):
    tok, feats = tokens.shape
    hid = weight.shape[1]
    fcol = weight.shape[0]
    nx, nz, _, ny, nc = SIZES
    ncol = 2 * ny * nc
    rfeat = feats // (nx * nz)
    xh, z, core = (lax.axis_index(a) for a in ("xh", "z", "core"))
    col = lax.axis_index(COL)
    token_count = tok * nx * nz

    own_cols = lax.dynamic_slice_in_dim(tokens, col * fcol, fcol, 1)
    half = exchange(jnp.broadcast_to(own_cols[None], (nz, tok, fcol)), "z")
    half = half.reshape(nz * tok, fcol)
    swap = [(0, 1), (1, 0)]
    own_weight = weight.T
    received = lax.ppermute(jnp.concatenate([own_weight, own_cols], axis=0), "xh", swap)
    other_weight, other_cols = received[:hid], received[hid:]

    halves = grad_in.reshape(2, tok, hid)
    from_a = lax.ppermute(jnp.where(xh == 0, halves[0], halves[1]), LEVEL, moves(0))
    from_b = lax.ppermute(jnp.where(xh == 0, halves[1], halves[0]), LEVEL, moves(1))
    own_first = core == xh
    cot = jnp.concatenate(
        [jnp.where(own_first, from_a, from_b), jnp.where(own_first, from_b, from_a)], axis=1
    )
    half, cot = lax.optimization_barrier((half, cot))

    both = jnp.concatenate([own_weight, other_weight], axis=0)
    part = lax.dot_general(half, both, (((1,), (1,)), ((), ())), preferred_element_type=jnp.float32)
    part = part.astype(jnp.bfloat16).reshape(ncol, tok, 2 * hid)
    pre_act = jnp.sum(exchange(part, COL).astype(jnp.float32), axis=0)
    slope = (cot.astype(jnp.float32) * silu_slope(pre_act)).astype(jnp.bfloat16)
    own, other = slope[:, :hid], slope[:, hid:]
    slope = jnp.stack([jnp.where(xh == 0, own, other), jnp.where(xh == 0, other, own)])
    wide = jnp.pad(slope, ((0, 0), (0, 0), (0, LANES - hid)))
    wide = to_tiles(wide)
    n_row = wide.shape[1]

    own_token = lax.dynamic_slice_in_dim(tokens, col, 1, 0).reshape(-1, 8, 128)
    pair = to_tiles(jnp.concatenate([slope[0], slope[1]], axis=1))
    sent = jnp.concatenate([pair, own_token, to_tiles(other_cols)], axis=0)
    n_slope, n_token = pair.shape[0], own_token.shape[0]
    lines = lax.all_gather(sent, "z", axis=0, tiled=False)
    blocks = from_tiles(lines[:, :n_slope], tok).reshape(nz // 2, 2, tok, 2 * hid)
    panels = jnp.stack(
        [
            jnp.concatenate([blocks[:, 0, :, :hid], blocks[:, 1, :, :hid]], axis=-1),
            jnp.concatenate([blocks[:, 0, :, hid:], blocks[:, 1, :, hid:]], axis=-1),
        ]
    )
    panels = to_tiles(panels.reshape(ncol, tok, 2 * hid))
    n_panel = panels.shape[1]
    panels = jnp.broadcast_to(panels[None], (nx, *panels.shape))

    rows = jnp.broadcast_to(wide[:, None], (nx, ncol, n_row, 8, 128))
    picked = lines[:, n_slope : n_slope + n_token].reshape(2, nz // 2, nx, nz, 2, 128)
    picked = lax.dynamic_index_in_dim(picked, z, 3, keepdims=False)
    picked = picked.transpose(2, 0, 3, 1, 4).reshape(nx, 1, 4, nz // 2, 128)
    picked = jnp.broadcast_to(picked, (nx, ncol, 4, nz // 2, 128))
    pieces = jnp.concatenate([panels, rows, picked], axis=2).reshape(nx * ncol, -1, 8, 128)
    pieces = exchange(pieces, LEVEL)

    panel = from_tiles(pieces[:, :n_panel], tok).reshape(-1, 2 * hid)
    row_block = from_tiles(pieces[:, n_panel : n_panel + n_row], tok).reshape(-1, LANES)[:, :hid]
    grad_cov = dot(row_block, panel) / token_count

    other_half = from_tiles(lines[:, n_slope + n_token :], tok).reshape(nz * tok, fcol)
    cols = jnp.stack([jnp.where(xh == 0, half, other_half), jnp.where(xh == 0, other_half, half)])
    cols = cols.reshape(nx, nz, tok, fcol).transpose(0, 2, 1, 3).reshape(-1, fcol)
    act_rows = pieces[:, n_panel + n_row :].reshape(nx * ncol, 2, 2, nz // 2, 128)
    act_rows = act_rows.transpose(0, 1, 3, 2, 4).reshape(-1, rfeat)
    act_cov = dot(act_rows, cols) / token_count
    return act_cov, grad_cov


def solution(mesh):
    fine = Mesh(mesh.devices.reshape(SIZES), ("xh", "z", "xl", "y", "core"))
    placed = (P(ROW, None), P(COL, ROW), P(COL, ROW))
    return jax.shard_map(
        shards,
        mesh=fine,
        in_specs=placed,
        out_specs=(P(ROW, COL), P(ROW, COL)),
        check_vma=False,
    )
```

```python
import jax
import jax.numpy as jnp
from jax import lax
from jax.sharding import Mesh, PartitionSpec as P

AXES = ("xh", "zq", "zp", "xl", "y", "core")
SIZES = (2, 8, 2, 2, 4, 2)
ROW = ("xh", "zq", "zp")
LINE = ("zq", "zp")
COL = ("xl", "y", "core")
LEVEL = ("xh", "xl", "y", "core")
LEVELS = ("xh", "zp", "xl", "y", "core")
CONTRACT = (((0,), (0,)), ((), ()))
LANES = 512


def exchange(parts, axis):
    return lax.all_to_all(parts, axis, split_axis=0, concat_axis=0, tiled=True)


def silu_slope(pre_act):
    sigmoid_value = jax.nn.sigmoid(pre_act)
    return sigmoid_value * (1.0 + pre_act * (1.0 - sigmoid_value))


def dot(a, b):
    return lax.dot_general(a, b, CONTRACT, preferred_element_type=jnp.float32)


def to_tiles(x):
    lead, (rows, lanes) = x.shape[:-2], x.shape[-2:]
    x = x.reshape(*lead, rows // 8, 8, lanes // 128, 128)
    return jnp.swapaxes(x, -3, -2).reshape(*lead, -1, 8, 128)


def from_tiles(x, rows):
    lead = x.shape[:-3]
    x = x.reshape(*lead, rows // 8, -1, 8, 128)
    return jnp.swapaxes(x, -3, -2).reshape(*lead, rows, -1)


def moves(source_bit):
    pairs = []
    for xh in range(2):
        for xl in range(2):
            for k in range(8):
                source = (xh * 2 + xl) * 8 + k
                core = xh if source_bit == 0 else 1 - xh
                pairs.append((source, ((xl * 2 + k // 4) * 4 + k % 4) * 2 + core))
    return pairs


def shards(tokens, weight, grad_in):
    tok, feats = tokens.shape
    hid = weight.shape[1]
    fcol = weight.shape[0]
    nx, nq, npar, _, ny, nc = SIZES
    nz = nq * npar
    ncol = 2 * ny * nc
    rfeat = feats // (nx * nz)
    xh, core = lax.axis_index("xh"), lax.axis_index("core")
    col = lax.axis_index(COL)
    token_count = tok * nx * nz

    own_cols = lax.dynamic_slice_in_dim(tokens, col * fcol, fcol, 1)
    own_token = lax.dynamic_slice_in_dim(tokens, col, 1, 0).reshape(nx, nq, npar, 2, rfeat // 2)
    own_token = own_token.transpose(1, 3, 0, 2, 4).reshape(nz, 1, nx * npar, rfeat // 2)
    own_token = jnp.pad(own_token, ((0, 0), (0, 0), (0, 8 - own_token.shape[2]), (0, 0)))
    sent = to_tiles(own_cols)
    n_cols = sent.shape[0]
    sent = jnp.concatenate([jnp.broadcast_to(sent[None], (nz, n_cols, 8, 128)), own_token], axis=1)
    gathered = exchange(sent, LINE)
    half = from_tiles(gathered[:, :n_cols], tok).reshape(nz * tok, fcol)
    picked = gathered[:, n_cols, : nx * npar].reshape(nz // 8, 8, nx, npar, rfeat // 2)
    picked = picked.transpose(2, 3, 0, 1, 4)
    swap = [(0, 1), (1, 0)]
    own_weight = weight.T
    other_weight = lax.ppermute(own_weight, "xh", swap)

    halves = grad_in.reshape(2, tok, hid)
    from_a = lax.ppermute(jnp.where(xh == 0, halves[0], halves[1]), LEVEL, moves(0))
    from_b = lax.ppermute(jnp.where(xh == 0, halves[1], halves[0]), LEVEL, moves(1))
    own_first = core == xh
    cot = jnp.concatenate(
        [jnp.where(own_first, from_a, from_b), jnp.where(own_first, from_b, from_a)], axis=1
    )
    half, cot = lax.optimization_barrier((half, cot))

    both = jnp.concatenate([own_weight, other_weight], axis=0)
    part = lax.dot_general(half, both, (((1,), (1,)), ((), ())), preferred_element_type=jnp.float32)
    part = part.astype(jnp.bfloat16).reshape(ncol, tok, 2 * hid)
    pre_act = jnp.sum(exchange(part, COL).astype(jnp.float32), axis=0)
    slope = (cot.astype(jnp.float32) * silu_slope(pre_act)).astype(jnp.bfloat16)
    own, other = slope[:, :hid], slope[:, hid:]
    pair = jnp.concatenate([jnp.where(xh == 0, own, other), jnp.where(xh == 0, other, own)], axis=1)

    few = tok // npar
    pair = to_tiles(pair.reshape(npar, few, 2 * hid))
    sent = jnp.broadcast_to(pair[None], (nq, *pair.shape)).reshape(nz, -1, 8, 128)
    lines = exchange(sent, LINE)
    other_half = lax.ppermute(half, "xh", swap)
    lines, other_half = lax.optimization_barrier((lines, other_half))
    blocks = from_tiles(lines, few).reshape(nq, npar, few, 2 * hid)

    panels = jnp.stack(
        [
            jnp.concatenate([blocks[:, 0, :, :hid], blocks[:, 1, :, :hid]], axis=-1),
            jnp.concatenate([blocks[:, 0, :, hid:], blocks[:, 1, :, hid:]], axis=-1),
        ]
    )
    panels = to_tiles(panels.reshape(ncol, few, 2 * hid))
    rows = lax.dynamic_index_in_dim(blocks, lax.axis_index("zq"), 0, keepdims=False)
    rows = jnp.stack([rows[:, :, :hid], rows[:, :, hid:]])
    rows = to_tiles(jnp.pad(rows, ((0, 0), (0, 0), (0, 0), (0, LANES - hid))))
    n_panel, n_row = panels.shape[1], rows.shape[2]
    lead = (nx, npar, ncol)
    pieces = jnp.concatenate(
        [
            jnp.broadcast_to(panels, (nx, npar, *panels.shape)),
            jnp.broadcast_to(rows[:, :, None], (*lead, n_row, 8, 128)),
            jnp.broadcast_to(picked[:, :, None], (*lead, nz // 8, 8, 128)),
        ],
        axis=3,
    )
    pieces = exchange(pieces.reshape(nx * npar * ncol, -1, 8, 128), LEVELS)

    panel = from_tiles(pieces[:, :n_panel], few).reshape(-1, 2 * hid)
    row_block = from_tiles(pieces[:, n_panel : n_panel + n_row], few).reshape(-1, LANES)[:, :hid]
    grad_cov = dot(row_block, panel) / token_count

    cols = jnp.stack([jnp.where(xh == 0, half, other_half), jnp.where(xh == 0, other_half, half)])
    cols = cols.reshape(nx, nz, tok, fcol).transpose(0, 2, 1, 3).reshape(-1, fcol)
    act_rows = pieces[:, n_panel + n_row :].reshape(nx, npar, ncol, nz, rfeat // 2)
    act_rows = act_rows.transpose(0, 2, 3, 1, 4).reshape(-1, rfeat)
    act_cov = dot(act_rows, cols) / token_count
    return act_cov, grad_cov


def solution(mesh):
    fine = Mesh(mesh.devices.reshape(SIZES), AXES)
    placed = (P(ROW, None), P(COL, ROW), P(COL, ROW))
    return jax.shard_map(
        shards,
        mesh=fine,
        in_specs=placed,
        out_specs=(P(ROW, COL), P(ROW, COL)),
        check_vma=False,
    )
```

```python
import jax
import jax.numpy as jnp
from jax import lax
from jax.sharding import Mesh, PartitionSpec as P

AXES = ("xh", "zq", "zp", "xl", "y", "core")
SIZES = (2, 8, 2, 2, 4, 2)
ROW = ("xh", "zq", "zp")
LINE = ("zq", "zp")
COL = ("xl", "y", "core")
LEVEL = ("xh", "xl", "y", "core")
LEVELS = ("xh", "zp", "xl", "y", "core")
CONTRACT = (((0,), (0,)), ((), ()))
LANES = 512


def exchange(parts, axis):
    return lax.all_to_all(parts, axis, split_axis=0, concat_axis=0, tiled=True)


def silu_slope(pre_act):
    sigmoid_value = jax.nn.sigmoid(pre_act)
    return sigmoid_value * (1.0 + pre_act * (1.0 - sigmoid_value))


def dot(a, b):
    return lax.dot_general(a, b, CONTRACT, preferred_element_type=jnp.float32)


def to_tiles(x):
    lead, (rows, lanes) = x.shape[:-2], x.shape[-2:]
    x = x.reshape(*lead, rows // 8, 8, lanes // 128, 128)
    return jnp.swapaxes(x, -3, -2).reshape(*lead, -1, 8, 128)


def from_tiles(x, rows):
    lead = x.shape[:-3]
    x = x.reshape(*lead, rows // 8, -1, 8, 128)
    return jnp.swapaxes(x, -3, -2).reshape(*lead, rows, -1)


def moves(source_bit):
    pairs = []
    for xh in range(2):
        for xl in range(2):
            for k in range(8):
                source = (xh * 2 + xl) * 8 + k
                core = xh if source_bit == 0 else 1 - xh
                pairs.append((source, ((xl * 2 + k // 4) * 4 + k % 4) * 2 + core))
    return pairs


def shards(tokens, weight, grad_in):
    tok, feats = tokens.shape
    hid = weight.shape[1]
    fcol = weight.shape[0]
    nx, nq, npar, _, ny, nc = SIZES
    nz = nq * npar
    ncol = 2 * ny * nc
    rfeat = feats // (nx * nz)
    xh, core = lax.axis_index("xh"), lax.axis_index("core")
    col = lax.axis_index(COL)
    token_count = tok * nx * nz

    own_cols = lax.dynamic_slice_in_dim(tokens, col * fcol, fcol, 1)
    own_token = lax.dynamic_slice_in_dim(tokens, col, 1, 0).reshape(nx, nq, npar, 2, rfeat // 2)
    own_token = own_token.transpose(1, 3, 0, 2, 4).reshape(nz, 1, nx * npar, rfeat // 2)
    own_token = jnp.pad(own_token, ((0, 0), (0, 0), (0, 8 - own_token.shape[2]), (0, 0)))
    sent = to_tiles(own_cols)
    n_cols = sent.shape[0]
    sent = jnp.concatenate([jnp.broadcast_to(sent[None], (nz, n_cols, 8, 128)), own_token], axis=1)
    gathered = exchange(sent, LINE)
    half = from_tiles(gathered[:, :n_cols], tok).reshape(nz * tok, fcol)
    picked = gathered[:, n_cols, : nx * npar].reshape(nz // 8, 8, nx, npar, rfeat // 2)
    picked = picked.transpose(2, 3, 0, 1, 4)
    swap = [(0, 1), (1, 0)]
    own_weight = weight.T
    other_weight = lax.ppermute(own_weight, "xh", swap)

    halves = grad_in.reshape(2, tok, hid)
    from_a = lax.ppermute(jnp.where(xh == 0, halves[0], halves[1]), LEVEL, moves(0))
    from_b = lax.ppermute(jnp.where(xh == 0, halves[1], halves[0]), LEVEL, moves(1))
    own_first = core == xh
    cot = jnp.concatenate(
        [jnp.where(own_first, from_a, from_b), jnp.where(own_first, from_b, from_a)], axis=1
    )
    half, cot = lax.optimization_barrier((half, cot))

    both = jnp.concatenate([own_weight, other_weight], axis=0)
    part = lax.dot_general(half, both, (((1,), (1,)), ((), ())), preferred_element_type=jnp.float32)
    part = part.astype(jnp.bfloat16).reshape(ncol, tok, 2 * hid)
    pre_act = jnp.sum(exchange(part, COL).astype(jnp.float32), axis=0)
    slope = (cot.astype(jnp.float32) * silu_slope(pre_act)).astype(jnp.bfloat16)
    own, other = slope[:, :hid], slope[:, hid:]
    pair = jnp.concatenate([jnp.where(xh == 0, own, other), jnp.where(xh == 0, other, own)], axis=1)

    few = tok // npar
    pair = to_tiles(pair.reshape(npar, few, 2 * hid))
    sent = jnp.broadcast_to(pair[None], (nq, *pair.shape)).reshape(nz, -1, 8, 128)
    lines = exchange(sent, LINE)
    other_half = lax.ppermute(half, "xh", swap)
    cols = jnp.stack([jnp.where(xh == 0, half, other_half), jnp.where(xh == 0, other_half, half)])
    cols = cols.reshape(nx, nz, tok, fcol).transpose(0, 2, 1, 3).reshape(-1, fcol)
    lines, cols = lax.optimization_barrier((lines, cols))
    blocks = from_tiles(lines, few).reshape(nq, npar, few, 2 * hid)

    panels = jnp.stack(
        [
            jnp.concatenate([blocks[:, 0, :, :hid], blocks[:, 1, :, :hid]], axis=-1),
            jnp.concatenate([blocks[:, 0, :, hid:], blocks[:, 1, :, hid:]], axis=-1),
        ]
    )
    panels = to_tiles(panels.reshape(ncol, few, 2 * hid))
    rows = lax.dynamic_index_in_dim(blocks, lax.axis_index("zq"), 0, keepdims=False)
    rows = jnp.stack([rows[:, :, :hid], rows[:, :, hid:]])
    rows = to_tiles(jnp.pad(rows, ((0, 0), (0, 0), (0, 0), (0, LANES - hid))))
    n_panel, n_row = panels.shape[1], rows.shape[2]
    lead = (nx, npar, ncol)
    pieces = jnp.concatenate(
        [
            jnp.broadcast_to(panels, (nx, npar, *panels.shape)),
            jnp.broadcast_to(rows[:, :, None], (*lead, n_row, 8, 128)),
            jnp.broadcast_to(picked[:, :, None], (*lead, nz // 8, 8, 128)),
        ],
        axis=3,
    )
    pieces = exchange(pieces.reshape(nx * npar * ncol, -1, 8, 128), LEVELS)

    panel = from_tiles(pieces[:, :n_panel], few).reshape(-1, 2 * hid)
    row_block = from_tiles(pieces[:, n_panel : n_panel + n_row], few).reshape(-1, LANES)[:, :hid]
    grad_cov = dot(row_block, panel) / token_count

    act_rows = pieces[:, n_panel + n_row :].reshape(nx, npar, ncol, nz, rfeat // 2)
    act_rows = act_rows.transpose(0, 2, 3, 1, 4).reshape(-1, rfeat)
    act_cov = dot(act_rows, cols) / token_count
    return act_cov, grad_cov


def solution(mesh):
    fine = Mesh(mesh.devices.reshape(SIZES), AXES)
    placed = (P(ROW, None), P(COL, ROW), P(COL, ROW))
    return jax.shard_map(
        shards,
        mesh=fine,
        in_specs=placed,
        out_specs=(P(ROW, COL), P(ROW, COL)),
        check_vma=False,
    )
```

```python
import functools

import jax
import jax.numpy as jnp
from jax import lax
from jax.experimental import pallas as pl
from jax.experimental.pallas import tpu as pltpu
from jax.sharding import Mesh, PartitionSpec as P

AXES = ("xh", "zq", "zp", "xl", "y", "core")
SIZES = (2, 8, 2, 2, 4, 2)
ROW = ("xh", "zq", "zp")
LINE = ("zq", "zp")
COL = ("xl", "y", "core")
LEVEL = ("xh", "xl", "y", "core")
LEVELS = ("xh", "zp", "xl", "y", "core")
CONTRACT = (((0,), (0,)), ((), ()))
LANES = 512


def exchange(parts, axis):
    return lax.all_to_all(parts, axis, split_axis=0, concat_axis=0, tiled=True)


def silu_slope(pre_act):
    sigmoid_value = jax.nn.sigmoid(pre_act)
    return sigmoid_value * (1.0 + pre_act * (1.0 - sigmoid_value))


def dot(a, b):
    return lax.dot_general(a, b, CONTRACT, preferred_element_type=jnp.float32)


def covariance_kernel(scale, rows_ref, panel_ref, act_rows_ref, cols_ref, grad_ref, act_ref, rows_t, act_t):
    step = pl.program_id(0)

    @pl.when(step == 0)
    def _():
        rows_t[...] = rows_ref[...].T
        act_t[...] = act_rows_ref[...].T

    for left, right, out in ((rows_t, panel_ref, grad_ref), (act_t, cols_ref, act_ref)):
        count = out.shape[0]
        mine = left[pl.ds(pl.multiple_of(step * count, count), count), :]
        out[...] = jnp.dot(mine, right[...], preferred_element_type=jnp.float32) * scale


def covariances(rows, panel, act_rows, cols, height, scale):
    steps = 2
    outs = [(height, panel.shape[1]), (act_rows.shape[1], cols.shape[1])]
    return pl.pallas_call(
        functools.partial(covariance_kernel, scale),
        grid=(steps,),
        in_specs=[pl.BlockSpec(memory_space=pltpu.VMEM)] * 4,
        out_specs=[pl.BlockSpec((m // steps, n), lambda i: (i, 0)) for m, n in outs],
        out_shape=[jax.ShapeDtypeStruct(shape, jnp.float32) for shape in outs],
        scratch_shapes=[
            pltpu.VMEM(rows.shape[::-1], rows.dtype),
            pltpu.VMEM(act_rows.shape[::-1], act_rows.dtype),
        ],
        compiler_params=pltpu.CompilerParams(vmem_limit_bytes=16 * 1024 * 1024),
    )(rows, panel, act_rows, cols)


def to_tiles(x):
    lead, (rows, lanes) = x.shape[:-2], x.shape[-2:]
    x = x.reshape(*lead, rows // 8, 8, lanes // 128, 128)
    return jnp.swapaxes(x, -3, -2).reshape(*lead, -1, 8, 128)


def from_tiles(x, rows):
    lead = x.shape[:-3]
    x = x.reshape(*lead, rows // 8, -1, 8, 128)
    return jnp.swapaxes(x, -3, -2).reshape(*lead, rows, -1)


def moves(source_bit):
    pairs = []
    for xh in range(2):
        for xl in range(2):
            for k in range(8):
                source = (xh * 2 + xl) * 8 + k
                core = xh if source_bit == 0 else 1 - xh
                pairs.append((source, ((xl * 2 + k // 4) * 4 + k % 4) * 2 + core))
    return pairs


def shards(tokens, weight, grad_in):
    tok, feats = tokens.shape
    hid = weight.shape[1]
    fcol = weight.shape[0]
    nx, nq, npar, _, ny, nc = SIZES
    nz = nq * npar
    ncol = 2 * ny * nc
    rfeat = feats // (nx * nz)
    xh, core = lax.axis_index("xh"), lax.axis_index("core")
    col = lax.axis_index(COL)
    token_count = tok * nx * nz

    own_cols = lax.dynamic_slice_in_dim(tokens, col * fcol, fcol, 1)
    own_token = lax.dynamic_slice_in_dim(tokens, col, 1, 0).reshape(nx, nq, npar, 2, rfeat // 2)
    own_token = own_token.transpose(1, 3, 0, 2, 4).reshape(nz, 1, nx * npar, rfeat // 2)
    own_token = jnp.pad(own_token, ((0, 0), (0, 0), (0, 8 - own_token.shape[2]), (0, 0)))
    sent = to_tiles(own_cols)
    n_cols = sent.shape[0]
    sent = jnp.concatenate([jnp.broadcast_to(sent[None], (nz, n_cols, 8, 128)), own_token], axis=1)
    gathered = exchange(sent, LINE)
    half = from_tiles(gathered[:, :n_cols], tok).reshape(nz * tok, fcol)
    picked = gathered[:, n_cols, : nx * npar].reshape(nz // 8, 8, nx, npar, rfeat // 2)
    picked = picked.transpose(2, 3, 0, 1, 4)
    swap = [(0, 1), (1, 0)]
    own_weight = weight.T
    other_weight = lax.ppermute(own_weight, "xh", swap)

    halves = grad_in.reshape(2, tok, hid)
    from_a = lax.ppermute(jnp.where(xh == 0, halves[0], halves[1]), LEVEL, moves(0))
    from_b = lax.ppermute(jnp.where(xh == 0, halves[1], halves[0]), LEVEL, moves(1))
    own_first = core == xh
    cot = jnp.concatenate(
        [jnp.where(own_first, from_a, from_b), jnp.where(own_first, from_b, from_a)], axis=1
    )
    half, cot = lax.optimization_barrier((half, cot))

    both = jnp.concatenate([own_weight, other_weight], axis=0)
    part = lax.dot_general(half, both, (((1,), (1,)), ((), ())), preferred_element_type=jnp.float32)
    part = part.astype(jnp.bfloat16).reshape(ncol, tok, 2 * hid)
    pre_act = jnp.sum(exchange(part, COL).astype(jnp.float32), axis=0)
    slope = (cot.astype(jnp.float32) * silu_slope(pre_act)).astype(jnp.bfloat16)
    own, other = slope[:, :hid], slope[:, hid:]
    pair = jnp.concatenate([jnp.where(xh == 0, own, other), jnp.where(xh == 0, other, own)], axis=1)

    few = tok // npar
    pair = to_tiles(pair.reshape(npar, few, 2 * hid))
    sent = jnp.broadcast_to(pair[None], (nq, *pair.shape)).reshape(nz, -1, 8, 128)
    lines = exchange(sent, LINE)
    other_half = lax.ppermute(half, "xh", swap)
    cols = jnp.stack([jnp.where(xh == 0, half, other_half), jnp.where(xh == 0, other_half, half)])
    cols = cols.reshape(nx, nz, tok, fcol).transpose(0, 2, 1, 3).reshape(-1, fcol)
    lines, cols = lax.optimization_barrier((lines, cols))
    blocks = from_tiles(lines, few).reshape(nq, npar, few, 2 * hid)

    panels = jnp.stack(
        [
            jnp.concatenate([blocks[:, 0, :, :hid], blocks[:, 1, :, :hid]], axis=-1),
            jnp.concatenate([blocks[:, 0, :, hid:], blocks[:, 1, :, hid:]], axis=-1),
        ]
    )
    panels = to_tiles(panels.reshape(ncol, few, 2 * hid))
    rows = lax.dynamic_index_in_dim(blocks, lax.axis_index("zq"), 0, keepdims=False)
    rows = jnp.stack([rows[:, :, :hid], rows[:, :, hid:]])
    rows = to_tiles(jnp.pad(rows, ((0, 0), (0, 0), (0, 0), (0, LANES - hid))))
    n_panel, n_row = panels.shape[1], rows.shape[2]
    lead = (nx, npar, ncol)
    pieces = jnp.concatenate(
        [
            jnp.broadcast_to(panels, (nx, npar, *panels.shape)),
            jnp.broadcast_to(rows[:, :, None], (*lead, n_row, 8, 128)),
            jnp.broadcast_to(picked[:, :, None], (*lead, nz // 8, 8, 128)),
        ],
        axis=3,
    )
    pieces = exchange(pieces.reshape(nx * npar * ncol, -1, 8, 128), LEVELS)

    panel = from_tiles(pieces[:, :n_panel], few).reshape(-1, 2 * hid)
    row_block = from_tiles(pieces[:, n_panel : n_panel + n_row], few).reshape(-1, LANES)
    act_rows = pieces[:, n_panel + n_row :].reshape(nx, npar, ncol, nz, rfeat // 2)
    act_rows = act_rows.transpose(0, 2, 3, 1, 4).reshape(-1, rfeat)
    grad_cov, act_cov = covariances(row_block, panel, act_rows, cols, hid, 1.0 / token_count)
    return act_cov, grad_cov


def solution(mesh):
    fine = Mesh(mesh.devices.reshape(SIZES), AXES)
    placed = (P(ROW, None), P(COL, ROW), P(COL, ROW))
    return jax.shard_map(
        shards,
        mesh=fine,
        in_specs=placed,
        out_specs=(P(ROW, COL), P(ROW, COL)),
        check_vma=False,
    )
```

```python
import functools

import jax
import jax.numpy as jnp
from jax import lax
from jax.experimental import pallas as pl
from jax.experimental.pallas import tpu as pltpu
from jax.sharding import Mesh, PartitionSpec as P

AXES = ("xh", "zq", "zp", "xl", "y", "core")
SIZES = (2, 8, 2, 2, 4, 2)
ROW = ("xh", "zq", "zp")
LINE = ("zq", "zp")
COL = ("xl", "y", "core")
LEVEL = ("xh", "xl", "y", "core")
LEVELS = ("xh", "zp", "xl", "y", "core")
CONTRACT = (((0,), (0,)), ((), ()))
LANES = 512


def exchange(parts, axis):
    return lax.all_to_all(parts, axis, split_axis=0, concat_axis=0, tiled=True)


def silu_slope(pre_act):
    sigmoid_value = jax.nn.sigmoid(pre_act)
    return sigmoid_value * (1.0 + pre_act * (1.0 - sigmoid_value))


def dot(a, b):
    return lax.dot_general(a, b, CONTRACT, preferred_element_type=jnp.float32)


def covariance_kernel(scale, rows_ref, panel_ref, act_rows_ref, cols_ref, grad_ref, act_ref, grad, act, act_t, sems):
    nx, halves, count, width = act_rows_ref.shape
    for x in range(nx):
        for h in range(halves):
            act_t[h * width : (h + 1) * width, x * count : (x + 1) * count] = act_rows_ref[x, h].T
    act[...] = jnp.dot(act_t[...], cols_ref[...], preferred_element_type=jnp.float32) * scale
    copies = [pltpu.make_async_copy(act, act_ref, sems.at[0])]
    copies[0].start()
    steps, height, _ = grad.shape
    rows_t = rows_ref[...].T
    for k in range(steps):
        mine = rows_t[k * height : (k + 1) * height]
        grad[k] = jnp.dot(mine, panel_ref[...], preferred_element_type=jnp.float32) * scale
        copy = pltpu.make_async_copy(grad.at[k], grad_ref.at[pl.ds(k * height, height)], sems.at[1 + k])
        copy.start()
        copies.append(copy)
    for copy in copies:
        copy.wait()


def covariances(rows, panel, act_rows, cols, height, scale):
    steps = 2
    grad_shape = (height, panel.shape[1])
    act_shape = (act_rows.shape[1] * act_rows.shape[3], cols.shape[1])
    return pl.pallas_call(
        functools.partial(covariance_kernel, scale),
        in_specs=[pl.BlockSpec(memory_space=pltpu.VMEM)] * 4,
        out_specs=[pl.BlockSpec(memory_space=pl.ANY)] * 2,
        out_shape=[jax.ShapeDtypeStruct(shape, jnp.float32) for shape in (grad_shape, act_shape)],
        scratch_shapes=[
            pltpu.VMEM((steps, height // steps, grad_shape[1]), jnp.float32),
            pltpu.VMEM(act_shape, jnp.float32),
            pltpu.VMEM((act_shape[0], cols.shape[0]), act_rows.dtype),
            pltpu.SemaphoreType.DMA((1 + steps,)),
        ],
        compiler_params=pltpu.CompilerParams(vmem_limit_bytes=16 * 1024 * 1024),
    )(rows, panel, act_rows, cols)


def to_tiles(x):
    lead, (rows, lanes) = x.shape[:-2], x.shape[-2:]
    x = x.reshape(*lead, rows // 8, 8, lanes // 128, 128)
    return jnp.swapaxes(x, -3, -2).reshape(*lead, -1, 8, 128)


def from_tiles(x, rows):
    lead = x.shape[:-3]
    x = x.reshape(*lead, rows // 8, -1, 8, 128)
    return jnp.swapaxes(x, -3, -2).reshape(*lead, rows, -1)


def moves(source_bit):
    pairs = []
    for xh in range(2):
        for xl in range(2):
            for k in range(8):
                source = (xh * 2 + xl) * 8 + k
                core = xh if source_bit == 0 else 1 - xh
                pairs.append((source, ((xl * 2 + k // 4) * 4 + k % 4) * 2 + core))
    return pairs


def shards(tokens, weight, grad_in):
    tok, feats = tokens.shape
    hid = weight.shape[1]
    fcol = weight.shape[0]
    nx, nq, npar, _, ny, nc = SIZES
    nz = nq * npar
    ncol = 2 * ny * nc
    rfeat = feats // (nx * nz)
    xh, core = lax.axis_index("xh"), lax.axis_index("core")
    col = lax.axis_index(COL)
    token_count = tok * nx * nz

    own_cols = lax.dynamic_slice_in_dim(tokens, col * fcol, fcol, 1)
    half = exchange(jnp.broadcast_to(own_cols[None], (nz, tok, fcol)), LINE)
    half = half.reshape(nz * tok, fcol)
    swap = [(0, 1), (1, 0)]
    own_weight = weight.T
    other_weight = lax.ppermute(own_weight, "xh", swap)

    halves = grad_in.reshape(2, tok, hid)
    from_a = lax.ppermute(jnp.where(xh == 0, halves[0], halves[1]), LEVEL, moves(0))
    from_b = lax.ppermute(jnp.where(xh == 0, halves[1], halves[0]), LEVEL, moves(1))
    own_first = core == xh
    cot = jnp.concatenate(
        [jnp.where(own_first, from_a, from_b), jnp.where(own_first, from_b, from_a)], axis=1
    )
    half, cot = lax.optimization_barrier((half, cot))

    both = jnp.concatenate([own_weight, other_weight], axis=0)
    part = lax.dot_general(half, both, (((1,), (1,)), ((), ())), preferred_element_type=jnp.float32)
    part = part.astype(jnp.bfloat16).reshape(ncol, tok, 2 * hid)
    pre_act = jnp.sum(exchange(part, COL).astype(jnp.float32), axis=0)
    slope = (cot.astype(jnp.float32) * silu_slope(pre_act)).astype(jnp.bfloat16)
    own, other = slope[:, :hid], slope[:, hid:]
    pair = jnp.concatenate([jnp.where(xh == 0, own, other), jnp.where(xh == 0, other, own)], axis=1)

    few = tok // npar
    own_token = lax.dynamic_slice_in_dim(tokens, col, 1, 0).reshape(nx, nq, npar, 2, rfeat // 2)
    own_token = own_token.transpose(1, 3, 0, 2, 4).reshape(nz, 1, nx * npar, rfeat // 2)
    own_token = jnp.pad(own_token, ((0, 0), (0, 0), (0, 8 - own_token.shape[2]), (0, 0)))
    pair = to_tiles(pair.reshape(npar, few, 2 * hid))
    n_pair = pair.shape[1]
    sent = jnp.broadcast_to(pair[None], (nq, *pair.shape)).reshape(nz, n_pair, 8, 128)
    gathered = exchange(jnp.concatenate([sent, own_token], axis=1), LINE)
    lines = gathered[:, :n_pair]
    picked = gathered[:, n_pair, : nx * npar].reshape(nz // 8, 8, nx, npar, rfeat // 2)
    picked = picked.transpose(2, 3, 0, 1, 4)
    other_half = lax.ppermute(half, "xh", swap)
    cols = jnp.stack([jnp.where(xh == 0, half, other_half), jnp.where(xh == 0, other_half, half)])
    cols = cols.reshape(nx, nz, tok, fcol).transpose(0, 2, 1, 3).reshape(-1, fcol)
    lines, picked, cols = lax.optimization_barrier((lines, picked, cols))
    blocks = from_tiles(lines, few).reshape(nq, npar, few, 2 * hid)

    panels = jnp.stack(
        [
            jnp.concatenate([blocks[:, 0, :, :hid], blocks[:, 1, :, :hid]], axis=-1),
            jnp.concatenate([blocks[:, 0, :, hid:], blocks[:, 1, :, hid:]], axis=-1),
        ]
    )
    panels = to_tiles(panels.reshape(ncol, few, 2 * hid))
    rows = lax.dynamic_index_in_dim(blocks, lax.axis_index("zq"), 0, keepdims=False)
    rows = jnp.stack([rows[:, :, :hid], rows[:, :, hid:]])
    rows = to_tiles(jnp.pad(rows, ((0, 0), (0, 0), (0, 0), (0, LANES - hid))))
    n_panel, n_row = panels.shape[1], rows.shape[2]
    lead = (nx, npar, ncol)
    pieces = jnp.concatenate(
        [
            jnp.broadcast_to(panels, (nx, npar, *panels.shape)),
            jnp.broadcast_to(rows[:, :, None], (*lead, n_row, 8, 128)),
            jnp.broadcast_to(picked[:, :, None], (*lead, nz // 8, 8, 128)),
        ],
        axis=3,
    )
    pieces = exchange(pieces.reshape(nx * npar * ncol, -1, 8, 128), LEVELS)

    panel = from_tiles(pieces[:, :n_panel], few).reshape(-1, 2 * hid)
    row_block = from_tiles(pieces[:, n_panel : n_panel + n_row], few).reshape(-1, LANES)
    act_rows = pieces[:, n_panel + n_row :].reshape(nx, npar, ncol * nz, rfeat // 2)
    grad_cov, act_cov = covariances(row_block, panel, act_rows, cols, hid, 1.0 / token_count)
    return act_cov, grad_cov


def solution(mesh):
    fine = Mesh(mesh.devices.reshape(SIZES), AXES)
    placed = (P(ROW, None), P(COL, ROW), P(COL, ROW))
    return jax.shard_map(
        shards,
        mesh=fine,
        in_specs=placed,
        out_specs=(P(ROW, COL), P(ROW, COL)),
        check_vma=False,
    )
```

```python
import functools

import jax
import jax.numpy as jnp
from jax import lax
from jax.experimental import pallas as pl
from jax.experimental.pallas import tpu as pltpu
from jax.sharding import Mesh, PartitionSpec as P

AXES = ("xh", "zq", "zp", "xl", "y", "core")
SIZES = (2, 8, 2, 2, 4, 2)
ROW = ("xh", "zq", "zp")
LINE = ("zq", "zp")
COL = ("xl", "y", "core")
LEVEL = ("xh", "xl", "y", "core")
LEVELS = ("xh", "zp", "xl", "y", "core")
CONTRACT = (((0,), (0,)), ((), ()))
LANES = 512


def exchange(parts, axis):
    return lax.all_to_all(parts, axis, split_axis=0, concat_axis=0, tiled=True)


def silu_slope(pre_act):
    sigmoid_value = jax.nn.sigmoid(pre_act)
    return sigmoid_value * (1.0 + pre_act * (1.0 - sigmoid_value))


def dot(a, b):
    return lax.dot_general(a, b, CONTRACT, preferred_element_type=jnp.float32)


def covariance_kernel(scale, rows_ref, panel_ref, act_rows_ref, cols_ref, grad_ref, act_ref, grad, act, act_t, sems):
    nx, halves, count, width = act_rows_ref.shape
    for x in range(nx):
        for h in range(halves):
            act_t[h * width : (h + 1) * width, x * count : (x + 1) * count] = act_rows_ref[x, h].T
    act[...] = jnp.dot(act_t[...], cols_ref[...], preferred_element_type=jnp.float32) * scale
    copies = [pltpu.make_async_copy(act, act_ref, sems.at[0])]
    copies[0].start()
    steps, height, _ = grad.shape
    rows_t = rows_ref[...].T
    for k in range(steps):
        mine = rows_t[k * height : (k + 1) * height]
        grad[k] = jnp.dot(mine, panel_ref[...], preferred_element_type=jnp.float32) * scale
        copy = pltpu.make_async_copy(grad.at[k], grad_ref.at[pl.ds(k * height, height)], sems.at[1 + k])
        copy.start()
        copies.append(copy)
    for copy in copies:
        copy.wait()


def covariances(rows, panel, act_rows, cols, height, scale):
    steps = 2
    grad_shape = (height, panel.shape[1])
    act_shape = (act_rows.shape[1] * act_rows.shape[3], cols.shape[1])
    return pl.pallas_call(
        functools.partial(covariance_kernel, scale),
        in_specs=[pl.BlockSpec(memory_space=pltpu.VMEM)] * 4,
        out_specs=[pl.BlockSpec(memory_space=pl.ANY)] * 2,
        out_shape=[jax.ShapeDtypeStruct(shape, jnp.float32) for shape in (grad_shape, act_shape)],
        scratch_shapes=[
            pltpu.VMEM((steps, height // steps, grad_shape[1]), jnp.float32),
            pltpu.VMEM(act_shape, jnp.float32),
            pltpu.VMEM((act_shape[0], cols.shape[0]), act_rows.dtype),
            pltpu.SemaphoreType.DMA((1 + steps,)),
        ],
        compiler_params=pltpu.CompilerParams(vmem_limit_bytes=16 * 1024 * 1024),
    )(rows, panel, act_rows, cols)


def to_tiles(x):
    lead, (rows, lanes) = x.shape[:-2], x.shape[-2:]
    x = x.reshape(*lead, rows // 8, 8, lanes // 128, 128)
    return jnp.swapaxes(x, -3, -2).reshape(*lead, -1, 8, 128)


def from_tiles(x, rows):
    lead = x.shape[:-3]
    x = x.reshape(*lead, rows // 8, -1, 8, 128)
    return jnp.swapaxes(x, -3, -2).reshape(*lead, rows, -1)


def moves(source_bit):
    pairs = []
    for xh in range(2):
        for xl in range(2):
            for k in range(8):
                source = (xh * 2 + xl) * 8 + k
                core = xh if source_bit == 0 else 1 - xh
                pairs.append((source, ((xl * 2 + k // 4) * 4 + k % 4) * 2 + core))
    return pairs


def shards(tokens, weight, grad_in):
    tok, feats = tokens.shape
    hid = weight.shape[1]
    fcol = weight.shape[0]
    nx, nq, npar, _, ny, nc = SIZES
    nz = nq * npar
    ncol = 2 * ny * nc
    rfeat = feats // (nx * nz)
    xh, core = lax.axis_index("xh"), lax.axis_index("core")
    col = lax.axis_index(COL)
    token_count = tok * nx * nz

    own_cols = lax.dynamic_slice_in_dim(tokens, col * fcol, fcol, 1)
    own_token = lax.dynamic_slice_in_dim(tokens, col, 1, 0).reshape(nx, nq, npar, 2, rfeat // 2)
    own_token = own_token.transpose(1, 3, 0, 2, 4).reshape(nz, 1, nx * npar, rfeat // 2)
    own_token = jnp.pad(own_token, ((0, 0), (0, 0), (0, 8 - own_token.shape[2]), (0, 0)))
    sent = to_tiles(own_cols)
    n_cols = sent.shape[0]
    sent = jnp.concatenate([jnp.broadcast_to(sent[None], (nz, n_cols, 8, 128)), own_token], axis=1)
    gathered = exchange(sent, LINE)
    half = from_tiles(gathered[:, :n_cols], tok).reshape(nz * tok, fcol)
    picked = gathered[:, n_cols, : nx * npar].reshape(nz // 8, 8, nx, npar, rfeat // 2)
    picked = picked.transpose(2, 3, 0, 1, 4)
    swap = [(0, 1), (1, 0)]
    own_weight = weight.T
    other_weight = lax.ppermute(own_weight, "xh", swap)

    halves = grad_in.reshape(2, tok, hid)
    from_a = lax.ppermute(jnp.where(xh == 0, halves[0], halves[1]), LEVEL, moves(0))
    from_b = lax.ppermute(jnp.where(xh == 0, halves[1], halves[0]), LEVEL, moves(1))
    own_first = core == xh
    cot = jnp.concatenate(
        [jnp.where(own_first, from_a, from_b), jnp.where(own_first, from_b, from_a)], axis=1
    )
    half, cot = lax.optimization_barrier((half, cot))

    both = jnp.concatenate([own_weight, other_weight], axis=0)
    part = lax.dot_general(half, both, (((1,), (1,)), ((), ())), preferred_element_type=jnp.float32)
    part = part.astype(jnp.bfloat16).reshape(ncol, tok, 2 * hid)
    pre_act = jnp.sum(exchange(part, COL).astype(jnp.float32), axis=0)
    slope = (cot.astype(jnp.float32) * silu_slope(pre_act)).astype(jnp.bfloat16)
    own, other = slope[:, :hid], slope[:, hid:]
    pair = jnp.concatenate([jnp.where(xh == 0, own, other), jnp.where(xh == 0, other, own)], axis=1)

    few = tok // npar
    pair = to_tiles(pair.reshape(npar, few, 2 * hid))
    sent = jnp.broadcast_to(pair[None], (nq, *pair.shape)).reshape(nz, -1, 8, 128)
    lines = exchange(sent, LINE)
    other_half = lax.ppermute(half, "xh", swap)
    cols = jnp.stack([jnp.where(xh == 0, half, other_half), jnp.where(xh == 0, other_half, half)])
    cols = cols.reshape(nx, nz, tok, fcol).transpose(0, 2, 1, 3).reshape(-1, fcol)
    lines, cols = lax.optimization_barrier((lines, cols))
    blocks = from_tiles(lines, few).reshape(nq, npar, few, 2 * hid)

    panels = jnp.stack(
        [
            jnp.concatenate([blocks[:, 0, :, :hid], blocks[:, 1, :, :hid]], axis=-1),
            jnp.concatenate([blocks[:, 0, :, hid:], blocks[:, 1, :, hid:]], axis=-1),
        ]
    )
    panels = to_tiles(panels.reshape(ncol, few, 2 * hid))
    rows = lax.dynamic_index_in_dim(blocks, lax.axis_index("zq"), 0, keepdims=False)
    rows = jnp.stack([rows[:, :, :hid], rows[:, :, hid:]])
    rows = to_tiles(jnp.pad(rows, ((0, 0), (0, 0), (0, 0), (0, LANES - hid))))
    n_panel, n_row = panels.shape[1], rows.shape[2]
    lead = (nx, npar, ncol)
    pieces = jnp.concatenate(
        [
            jnp.broadcast_to(panels, (nx, npar, *panels.shape)),
            jnp.broadcast_to(rows[:, :, None], (*lead, n_row, 8, 128)),
            jnp.broadcast_to(picked[:, :, None], (*lead, nz // 8, 8, 128)),
        ],
        axis=3,
    )
    pieces = exchange(pieces.reshape(nx * npar * ncol, -1, 8, 128), LEVELS)

    panel = from_tiles(pieces[:, :n_panel], few).reshape(-1, 2 * hid)
    row_block = from_tiles(pieces[:, n_panel : n_panel + n_row], few).reshape(-1, LANES)
    act_rows = pieces[:, n_panel + n_row :].reshape(nx, npar, ncol * nz, rfeat // 2)
    grad_cov, act_cov = covariances(row_block, panel, act_rows, cols, hid, 1.0 / token_count)
    return act_cov, grad_cov


def solution(mesh):
    fine = Mesh(mesh.devices.reshape(SIZES), AXES)
    placed = (P(ROW, None), P(COL, ROW), P(COL, ROW))
    return jax.shard_map(
        shards,
        mesh=fine,
        in_specs=placed,
        out_specs=(P(ROW, COL), P(ROW, COL)),
        check_vma=False,
    )
```

```python
import functools

import jax
import jax.numpy as jnp
from jax import lax
from jax.experimental import pallas as pl
from jax.experimental.pallas import tpu as pltpu
from jax.sharding import Mesh, PartitionSpec as P

AXES = ("xh", "zq", "zp", "xl", "y", "core")
SIZES = (2, 8, 2, 2, 4, 2)
ROW = ("xh", "zq", "zp")
LINE = ("zq", "zp")
COL = ("xl", "y", "core")
LEVEL = ("xh", "xl", "y", "core")
LEVELS = ("xh", "zp", "xl", "y", "core")
CONTRACT = (((0,), (0,)), ((), ()))
LANES = 512


def exchange(parts, axis):
    return lax.all_to_all(parts, axis, split_axis=0, concat_axis=0, tiled=True)


def silu_slope(pre_act):
    sigmoid_value = jax.nn.sigmoid(pre_act)
    return sigmoid_value * (1.0 + pre_act * (1.0 - sigmoid_value))


def dot(a, b):
    return lax.dot_general(a, b, CONTRACT, preferred_element_type=jnp.float32)


def covariance_kernel(scale, rows_ref, panel_ref, act_rows_ref, cols_ref, grad_ref, act_ref, grad, act, act_t, sems):
    nx, halves, count, width = act_rows_ref.shape
    for x in range(nx):
        for h in range(halves):
            act_t[h * width : (h + 1) * width, x * count : (x + 1) * count] = act_rows_ref[x, h].T
    act[...] = jnp.dot(act_t[...], cols_ref[...], preferred_element_type=jnp.float32) * scale
    copies = [pltpu.make_async_copy(act, act_ref, sems.at[0])]
    copies[0].start()
    steps, height, _ = grad.shape
    rows_t = rows_ref[...].T
    for k in range(steps):
        mine = rows_t[k * height : (k + 1) * height]
        grad[k] = jnp.dot(mine, panel_ref[...], preferred_element_type=jnp.float32) * scale
        copy = pltpu.make_async_copy(grad.at[k], grad_ref.at[pl.ds(k * height, height)], sems.at[1 + k])
        copy.start()
        copies.append(copy)
    for copy in copies:
        copy.wait()


def covariances(rows, panel, act_rows, cols, height, scale):
    steps = 2
    grad_shape = (height, panel.shape[1])
    act_shape = (act_rows.shape[1] * act_rows.shape[3], cols.shape[1])
    return pl.pallas_call(
        functools.partial(covariance_kernel, scale),
        in_specs=[pl.BlockSpec(memory_space=pltpu.VMEM)] * 4,
        out_specs=[pl.BlockSpec(memory_space=pl.ANY)] * 2,
        out_shape=[jax.ShapeDtypeStruct(shape, jnp.float32) for shape in (grad_shape, act_shape)],
        scratch_shapes=[
            pltpu.VMEM((steps, height // steps, grad_shape[1]), jnp.float32),
            pltpu.VMEM(act_shape, jnp.float32),
            pltpu.VMEM((act_shape[0], cols.shape[0]), act_rows.dtype),
            pltpu.SemaphoreType.DMA((1 + steps,)),
        ],
        compiler_params=pltpu.CompilerParams(vmem_limit_bytes=16 * 1024 * 1024),
    )(rows, panel, act_rows, cols)


def to_tiles(x):
    lead, (rows, lanes) = x.shape[:-2], x.shape[-2:]
    x = x.reshape(*lead, rows // 8, 8, lanes // 128, 128)
    return jnp.swapaxes(x, -3, -2).reshape(*lead, -1, 8, 128)


def from_tiles(x, rows):
    lead = x.shape[:-3]
    x = x.reshape(*lead, rows // 8, -1, 8, 128)
    return jnp.swapaxes(x, -3, -2).reshape(*lead, rows, -1)


def moves(source_bit):
    pairs = []
    for xh in range(2):
        for xl in range(2):
            for k in range(8):
                source = (xh * 2 + xl) * 8 + k
                core = xh if source_bit == 0 else 1 - xh
                pairs.append((source, ((xl * 2 + k // 4) * 4 + k % 4) * 2 + core))
    return pairs


def shards(tokens, weight, grad_in):
    tok, feats = tokens.shape
    hid = weight.shape[1]
    fcol = weight.shape[0]
    nx, nq, npar, _, ny, nc = SIZES
    nz = nq * npar
    ncol = 2 * ny * nc
    rfeat = feats // (nx * nz)
    xh, core = lax.axis_index("xh"), lax.axis_index("core")
    col = lax.axis_index(COL)
    token_count = tok * nx * nz

    own_cols = lax.dynamic_slice_in_dim(tokens, col * fcol, fcol, 1)
    own_token = lax.dynamic_slice_in_dim(tokens, col, 1, 0).reshape(nx, nq, npar, 2, rfeat // 2)
    own_token = own_token.transpose(1, 3, 0, 2, 4).reshape(nz, 1, nx * npar, rfeat // 2)
    own_token = jnp.pad(own_token, ((0, 0), (0, 0), (0, 8 - own_token.shape[2]), (0, 0)))
    sent = to_tiles(own_cols)
    n_cols = sent.shape[0]
    sent = jnp.concatenate([jnp.broadcast_to(sent[None], (nz, n_cols, 8, 128)), own_token], axis=1)
    gathered = exchange(sent, LINE)
    half = from_tiles(gathered[:, :n_cols], tok).reshape(nz * tok, fcol)
    picked = gathered[:, n_cols, : nx * npar].reshape(nz // 8, 8, nx, npar, rfeat // 2)
    picked = picked.transpose(2, 3, 0, 1, 4)
    swap = [(0, 1), (1, 0)]
    own_weight = weight.T
    other_weight = lax.ppermute(own_weight, "xh", swap)

    halves = grad_in.reshape(2, tok, hid)
    from_a = lax.ppermute(jnp.where(xh == 0, halves[0], halves[1]), LEVEL, moves(0))
    from_b = lax.ppermute(jnp.where(xh == 0, halves[1], halves[0]), LEVEL, moves(1))
    own_first = core == xh
    cot = jnp.concatenate(
        [jnp.where(own_first, from_a, from_b), jnp.where(own_first, from_b, from_a)], axis=1
    )
    half, cot = lax.optimization_barrier((half, cot))

    both = jnp.concatenate([own_weight, other_weight], axis=0)
    part = lax.dot_general(half, both, (((1,), (1,)), ((), ())), preferred_element_type=jnp.float32)
    part = part.reshape(ncol, tok, 2 * hid)
    pre_act = jnp.sum(exchange(part, COL), axis=0)
    slope = (cot.astype(jnp.float32) * silu_slope(pre_act)).astype(jnp.bfloat16)
    own, other = slope[:, :hid], slope[:, hid:]
    pair = jnp.concatenate([jnp.where(xh == 0, own, other), jnp.where(xh == 0, other, own)], axis=1)

    few = tok // npar
    pair = to_tiles(pair.reshape(npar, few, 2 * hid))
    sent = jnp.broadcast_to(pair[None], (nq, *pair.shape)).reshape(nz, -1, 8, 128)
    lines = exchange(sent, LINE)
    other_half = lax.ppermute(half, "xh", swap)
    cols = jnp.stack([jnp.where(xh == 0, half, other_half), jnp.where(xh == 0, other_half, half)])
    cols = cols.reshape(nx, nz, tok, fcol).transpose(0, 2, 1, 3).reshape(-1, fcol)
    lines, cols = lax.optimization_barrier((lines, cols))
    blocks = from_tiles(lines, few).reshape(nq, npar, few, 2 * hid)

    panels = jnp.stack(
        [
            jnp.concatenate([blocks[:, 0, :, :hid], blocks[:, 1, :, :hid]], axis=-1),
            jnp.concatenate([blocks[:, 0, :, hid:], blocks[:, 1, :, hid:]], axis=-1),
        ]
    )
    panels = to_tiles(panels.reshape(ncol, few, 2 * hid))
    rows = lax.dynamic_index_in_dim(blocks, lax.axis_index("zq"), 0, keepdims=False)
    rows = jnp.stack([rows[:, :, :hid], rows[:, :, hid:]])
    rows = to_tiles(jnp.pad(rows, ((0, 0), (0, 0), (0, 0), (0, LANES - hid))))
    n_panel, n_row = panels.shape[1], rows.shape[2]
    lead = (nx, npar, ncol)
    pieces = jnp.concatenate(
        [
            jnp.broadcast_to(panels, (nx, npar, *panels.shape)),
            jnp.broadcast_to(rows[:, :, None], (*lead, n_row, 8, 128)),
            jnp.broadcast_to(picked[:, :, None], (*lead, nz // 8, 8, 128)),
        ],
        axis=3,
    )
    pieces = exchange(pieces.reshape(nx * npar * ncol, -1, 8, 128), LEVELS)

    panel = from_tiles(pieces[:, :n_panel], few).reshape(-1, 2 * hid)
    row_block = from_tiles(pieces[:, n_panel : n_panel + n_row], few).reshape(-1, LANES)
    act_rows = pieces[:, n_panel + n_row :].reshape(nx, npar, ncol * nz, rfeat // 2)
    grad_cov, act_cov = covariances(row_block, panel, act_rows, cols, hid, 1.0 / token_count)
    return act_cov, grad_cov


def solution(mesh):
    fine = Mesh(mesh.devices.reshape(SIZES), AXES)
    placed = (P(ROW, None), P(COL, ROW), P(COL, ROW))
    return jax.shard_map(
        shards,
        mesh=fine,
        in_specs=placed,
        out_specs=(P(ROW, COL), P(ROW, COL)),
        check_vma=False,
    )
```

```python
import functools

import jax
import jax.numpy as jnp
from jax import lax
from jax.experimental import pallas as pl
from jax.experimental.pallas import tpu as pltpu
from jax.sharding import Mesh, PartitionSpec as P

AXES = ("xh", "zq", "zp", "xl", "y", "core")
SIZES = (2, 8, 2, 2, 4, 2)
ROW = ("xh", "zq", "zp")
LINE = ("zq", "zp")
COL = ("xl", "y", "core")
LEVEL = ("xh", "xl", "y", "core")
LEVELS = ("xh", "zp", "xl", "y", "core")
CONTRACT = (((0,), (0,)), ((), ()))
LANES = 512


def exchange(parts, axis):
    return lax.all_to_all(parts, axis, split_axis=0, concat_axis=0, tiled=True)


def silu_slope(pre_act):
    sigmoid_value = jax.nn.sigmoid(pre_act)
    return sigmoid_value * (1.0 + pre_act * (1.0 - sigmoid_value))


def dot(a, b):
    return lax.dot_general(a, b, CONTRACT, preferred_element_type=jnp.float32)


def covariance_kernel(scale, rows_ref, panel_ref, act_rows_ref, cols_ref, grad_ref, act_ref, grad, act, act_t, sems):
    steps, height, _ = grad.shape
    copies = []
    rows_t = rows_ref[...].T
    for k in range(steps):
        mine = rows_t[k * height : (k + 1) * height]
        grad[k] = jnp.dot(mine, panel_ref[...], preferred_element_type=jnp.float32) * scale
        copy = pltpu.make_async_copy(grad.at[k], grad_ref.at[pl.ds(k * height, height)], sems.at[1 + k])
        copy.start()
        copies.append(copy)
    nx, halves, count, width = act_rows_ref.shape
    for x in range(nx):
        for h in range(halves):
            act_t[h * width : (h + 1) * width, x * count : (x + 1) * count] = act_rows_ref[x, h].T
    act[...] = jnp.dot(act_t[...], cols_ref[...], preferred_element_type=jnp.float32) * scale
    copies.append(pltpu.make_async_copy(act, act_ref, sems.at[0]))
    copies[-1].start()
    for copy in copies:
        copy.wait()


def covariances(rows, panel, act_rows, cols, height, scale):
    steps = 2
    grad_shape = (height, panel.shape[1])
    act_shape = (act_rows.shape[1] * act_rows.shape[3], cols.shape[1])
    return pl.pallas_call(
        functools.partial(covariance_kernel, scale),
        in_specs=[pl.BlockSpec(memory_space=pltpu.VMEM)] * 4,
        out_specs=[pl.BlockSpec(memory_space=pl.ANY)] * 2,
        out_shape=[jax.ShapeDtypeStruct(shape, jnp.float32) for shape in (grad_shape, act_shape)],
        scratch_shapes=[
            pltpu.VMEM((steps, height // steps, grad_shape[1]), jnp.float32),
            pltpu.VMEM(act_shape, jnp.float32),
            pltpu.VMEM((act_shape[0], cols.shape[0]), act_rows.dtype),
            pltpu.SemaphoreType.DMA((1 + steps,)),
        ],
        compiler_params=pltpu.CompilerParams(vmem_limit_bytes=16 * 1024 * 1024),
    )(rows, panel, act_rows, cols)


def to_tiles(x):
    lead, (rows, lanes) = x.shape[:-2], x.shape[-2:]
    x = x.reshape(*lead, rows // 8, 8, lanes // 128, 128)
    return jnp.swapaxes(x, -3, -2).reshape(*lead, -1, 8, 128)


def from_tiles(x, rows):
    lead = x.shape[:-3]
    x = x.reshape(*lead, rows // 8, -1, 8, 128)
    return jnp.swapaxes(x, -3, -2).reshape(*lead, rows, -1)


def moves(source_bit):
    pairs = []
    for xh in range(2):
        for xl in range(2):
            for k in range(8):
                source = (xh * 2 + xl) * 8 + k
                core = xh if source_bit == 0 else 1 - xh
                pairs.append((source, ((xl * 2 + k // 4) * 4 + k % 4) * 2 + core))
    return pairs


def shards(tokens, weight, grad_in):
    tok, feats = tokens.shape
    hid = weight.shape[1]
    fcol = weight.shape[0]
    nx, nq, npar, _, ny, nc = SIZES
    nz = nq * npar
    ncol = 2 * ny * nc
    rfeat = feats // (nx * nz)
    xh, core = lax.axis_index("xh"), lax.axis_index("core")
    col = lax.axis_index(COL)
    token_count = tok * nx * nz

    own_cols = lax.dynamic_slice_in_dim(tokens, col * fcol, fcol, 1)
    own_token = lax.dynamic_slice_in_dim(tokens, col, 1, 0).reshape(nx, nq, npar, 2, rfeat // 2)
    own_token = own_token.transpose(1, 3, 0, 2, 4).reshape(nz, 1, nx * npar, rfeat // 2)
    own_token = jnp.pad(own_token, ((0, 0), (0, 0), (0, 8 - own_token.shape[2]), (0, 0)))
    sent = to_tiles(own_cols)
    n_cols = sent.shape[0]
    sent = jnp.concatenate([jnp.broadcast_to(sent[None], (nz, n_cols, 8, 128)), own_token], axis=1)
    gathered = exchange(sent, LINE)
    half = from_tiles(gathered[:, :n_cols], tok).reshape(nz * tok, fcol)
    picked = gathered[:, n_cols, : nx * npar].reshape(nz // 8, 8, nx, npar, rfeat // 2)
    picked = picked.transpose(2, 3, 0, 1, 4)
    swap = [(0, 1), (1, 0)]
    own_weight = weight.T
    other_weight = lax.ppermute(own_weight, "xh", swap)

    halves = grad_in.reshape(2, tok, hid)
    from_a = lax.ppermute(jnp.where(xh == 0, halves[0], halves[1]), LEVEL, moves(0))
    from_b = lax.ppermute(jnp.where(xh == 0, halves[1], halves[0]), LEVEL, moves(1))
    own_first = core == xh
    cot = jnp.concatenate(
        [jnp.where(own_first, from_a, from_b), jnp.where(own_first, from_b, from_a)], axis=1
    )
    half, cot = lax.optimization_barrier((half, cot))

    both = jnp.concatenate([own_weight, other_weight], axis=0)
    part = lax.dot_general(half, both, (((1,), (1,)), ((), ())), preferred_element_type=jnp.float32)
    part = part.astype(jnp.bfloat16).reshape(ncol, tok, 2 * hid)
    pre_act = jnp.sum(exchange(part, COL).astype(jnp.float32), axis=0)
    slope = (cot.astype(jnp.float32) * silu_slope(pre_act)).astype(jnp.bfloat16)
    own, other = slope[:, :hid], slope[:, hid:]
    pair = jnp.concatenate([jnp.where(xh == 0, own, other), jnp.where(xh == 0, other, own)], axis=1)

    few = tok // npar
    pair = to_tiles(pair.reshape(npar, few, 2 * hid))
    sent = jnp.broadcast_to(pair[None], (nq, *pair.shape)).reshape(nz, -1, 8, 128)
    lines = exchange(sent, LINE)
    other_half = lax.ppermute(half, "xh", swap)
    cols = jnp.stack([jnp.where(xh == 0, half, other_half), jnp.where(xh == 0, other_half, half)])
    cols = cols.reshape(nx, nz, tok, fcol).transpose(0, 2, 1, 3).reshape(-1, fcol)
    lines, cols = lax.optimization_barrier((lines, cols))
    blocks = from_tiles(lines, few).reshape(nq, npar, few, 2 * hid)

    panels = jnp.stack(
        [
            jnp.concatenate([blocks[:, 0, :, :hid], blocks[:, 1, :, :hid]], axis=-1),
            jnp.concatenate([blocks[:, 0, :, hid:], blocks[:, 1, :, hid:]], axis=-1),
        ]
    )
    panels = to_tiles(panels.reshape(ncol, few, 2 * hid))
    rows = lax.dynamic_index_in_dim(blocks, lax.axis_index("zq"), 0, keepdims=False)
    rows = jnp.stack([rows[:, :, :hid], rows[:, :, hid:]])
    rows = to_tiles(jnp.pad(rows, ((0, 0), (0, 0), (0, 0), (0, LANES - hid))))
    n_panel, n_row = panels.shape[1], rows.shape[2]
    lead = (nx, npar, ncol)
    pieces = jnp.concatenate(
        [
            jnp.broadcast_to(panels, (nx, npar, *panels.shape)),
            jnp.broadcast_to(rows[:, :, None], (*lead, n_row, 8, 128)),
            jnp.broadcast_to(picked[:, :, None], (*lead, nz // 8, 8, 128)),
        ],
        axis=3,
    )
    pieces = exchange(pieces.reshape(nx * npar * ncol, -1, 8, 128), LEVELS)

    panel = from_tiles(pieces[:, :n_panel], few).reshape(-1, 2 * hid)
    row_block = from_tiles(pieces[:, n_panel : n_panel + n_row], few).reshape(-1, LANES)
    act_rows = pieces[:, n_panel + n_row :].reshape(nx, npar, ncol * nz, rfeat // 2)
    grad_cov, act_cov = covariances(row_block, panel, act_rows, cols, hid, 1.0 / token_count)
    return act_cov, grad_cov


def solution(mesh):
    fine = Mesh(mesh.devices.reshape(SIZES), AXES)
    placed = (P(ROW, None), P(COL, ROW), P(COL, ROW))
    return jax.shard_map(
        shards,
        mesh=fine,
        in_specs=placed,
        out_specs=(P(ROW, COL), P(ROW, COL)),
        check_vma=False,
    )
```

```python
import functools

import jax
import jax.numpy as jnp
from jax import lax
from jax.experimental import pallas as pl
from jax.experimental.pallas import tpu as pltpu
from jax.sharding import Mesh, PartitionSpec as P

AXES = ("xh", "zq", "zp", "xl", "y", "core")
SIZES = (2, 8, 2, 2, 4, 2)
ROW = ("xh", "zq", "zp")
LINE = ("zq", "zp")
COL = ("xl", "y", "core")
LEVEL = ("xh", "xl", "y", "core")
LEVELS = ("xh", "zp", "xl", "y", "core")
CONTRACT = (((0,), (0,)), ((), ()))
LANES = 512


def exchange(parts, axis):
    return lax.all_to_all(parts, axis, split_axis=0, concat_axis=0, tiled=True)


def silu_slope(pre_act):
    sigmoid_value = jax.nn.sigmoid(pre_act)
    return sigmoid_value * (1.0 + pre_act * (1.0 - sigmoid_value))


def dot(a, b):
    return lax.dot_general(a, b, CONTRACT, preferred_element_type=jnp.float32)


def covariance_kernel(scale, rows_ref, panel_ref, act_rows_ref, cols_ref, grad_ref, act_ref, grad, act, act_t, sems):
    steps, height, _ = grad.shape
    copies = []
    rows_t = rows_ref[...].T
    for k in range(steps):
        mine = rows_t[k * height : (k + 1) * height]
        grad[k] = jnp.dot(mine, panel_ref[...], preferred_element_type=jnp.float32) * scale
        copy = pltpu.make_async_copy(grad.at[k], grad_ref.at[pl.ds(k * height, height)], sems.at[1 + k])
        copy.start()
        copies.append(copy)
    nx, halves, count, width = act_rows_ref.shape
    for x in range(nx):
        for h in range(halves):
            act_t[h * width : (h + 1) * width, x * count : (x + 1) * count] = act_rows_ref[x, h].T
    act[...] = jnp.dot(act_t[...], cols_ref[...], preferred_element_type=jnp.float32) * scale
    copies.append(pltpu.make_async_copy(act, act_ref, sems.at[0]))
    copies[-1].start()
    for copy in copies:
        copy.wait()


def covariances(rows, panel, act_rows, cols, height, scale):
    steps = 1
    grad_shape = (height, panel.shape[1])
    act_shape = (act_rows.shape[1] * act_rows.shape[3], cols.shape[1])
    return pl.pallas_call(
        functools.partial(covariance_kernel, scale),
        in_specs=[pl.BlockSpec(memory_space=pltpu.VMEM)] * 4,
        out_specs=[pl.BlockSpec(memory_space=pl.ANY)] * 2,
        out_shape=[jax.ShapeDtypeStruct(shape, jnp.float32) for shape in (grad_shape, act_shape)],
        scratch_shapes=[
            pltpu.VMEM((steps, height // steps, grad_shape[1]), jnp.float32),
            pltpu.VMEM(act_shape, jnp.float32),
            pltpu.VMEM((act_shape[0], cols.shape[0]), act_rows.dtype),
            pltpu.SemaphoreType.DMA((1 + steps,)),
        ],
        compiler_params=pltpu.CompilerParams(vmem_limit_bytes=16 * 1024 * 1024),
    )(rows, panel, act_rows, cols)


def to_tiles(x):
    lead, (rows, lanes) = x.shape[:-2], x.shape[-2:]
    x = x.reshape(*lead, rows // 8, 8, lanes // 128, 128)
    return jnp.swapaxes(x, -3, -2).reshape(*lead, -1, 8, 128)


def from_tiles(x, rows):
    lead = x.shape[:-3]
    x = x.reshape(*lead, rows // 8, -1, 8, 128)
    return jnp.swapaxes(x, -3, -2).reshape(*lead, rows, -1)


def moves(source_bit):
    pairs = []
    for xh in range(2):
        for xl in range(2):
            for k in range(8):
                source = (xh * 2 + xl) * 8 + k
                core = xh if source_bit == 0 else 1 - xh
                pairs.append((source, ((xl * 2 + k // 4) * 4 + k % 4) * 2 + core))
    return pairs


def shards(tokens, weight, grad_in):
    tok, feats = tokens.shape
    hid = weight.shape[1]
    fcol = weight.shape[0]
    nx, nq, npar, _, ny, nc = SIZES
    nz = nq * npar
    ncol = 2 * ny * nc
    rfeat = feats // (nx * nz)
    xh, core = lax.axis_index("xh"), lax.axis_index("core")
    col = lax.axis_index(COL)
    token_count = tok * nx * nz

    own_cols = lax.dynamic_slice_in_dim(tokens, col * fcol, fcol, 1)
    own_token = lax.dynamic_slice_in_dim(tokens, col, 1, 0).reshape(nx, nq, npar, 2, rfeat // 2)
    own_token = own_token.transpose(1, 3, 0, 2, 4).reshape(nz, 1, nx * npar, rfeat // 2)
    own_token = jnp.pad(own_token, ((0, 0), (0, 0), (0, 8 - own_token.shape[2]), (0, 0)))
    sent = to_tiles(own_cols)
    n_cols = sent.shape[0]
    sent = jnp.concatenate([jnp.broadcast_to(sent[None], (nz, n_cols, 8, 128)), own_token], axis=1)
    gathered = exchange(sent, LINE)
    half = from_tiles(gathered[:, :n_cols], tok).reshape(nz * tok, fcol)
    picked = gathered[:, n_cols, : nx * npar].reshape(nz // 8, 8, nx, npar, rfeat // 2)
    picked = picked.transpose(2, 3, 0, 1, 4)
    swap = [(0, 1), (1, 0)]
    own_weight = weight.T
    other_weight = lax.ppermute(own_weight, "xh", swap)

    halves = grad_in.reshape(2, tok, hid)
    from_a = lax.ppermute(jnp.where(xh == 0, halves[0], halves[1]), LEVEL, moves(0))
    from_b = lax.ppermute(jnp.where(xh == 0, halves[1], halves[0]), LEVEL, moves(1))
    own_first = core == xh
    cot = jnp.concatenate(
        [jnp.where(own_first, from_a, from_b), jnp.where(own_first, from_b, from_a)], axis=1
    )
    half, cot = lax.optimization_barrier((half, cot))

    both = jnp.concatenate([own_weight, other_weight], axis=0)
    part = lax.dot_general(half, both, (((1,), (1,)), ((), ())), preferred_element_type=jnp.float32)
    part = part.astype(jnp.bfloat16).reshape(ncol, tok, 2 * hid)
    pre_act = jnp.sum(exchange(part, COL).astype(jnp.float32), axis=0)
    slope = (cot.astype(jnp.float32) * silu_slope(pre_act)).astype(jnp.bfloat16)
    own, other = slope[:, :hid], slope[:, hid:]
    pair = jnp.concatenate([jnp.where(xh == 0, own, other), jnp.where(xh == 0, other, own)], axis=1)

    few = tok // npar
    pair = to_tiles(pair.reshape(npar, few, 2 * hid))
    sent = jnp.broadcast_to(pair[None], (nq, *pair.shape)).reshape(nz, -1, 8, 128)
    lines = exchange(sent, LINE)
    other_half = lax.ppermute(half, "xh", swap)
    cols = jnp.stack([jnp.where(xh == 0, half, other_half), jnp.where(xh == 0, other_half, half)])
    cols = cols.reshape(nx, nz, tok, fcol).transpose(0, 2, 1, 3).reshape(-1, fcol)
    lines, cols = lax.optimization_barrier((lines, cols))
    blocks = from_tiles(lines, few).reshape(nq, npar, few, 2 * hid)

    panels = jnp.stack(
        [
            jnp.concatenate([blocks[:, 0, :, :hid], blocks[:, 1, :, :hid]], axis=-1),
            jnp.concatenate([blocks[:, 0, :, hid:], blocks[:, 1, :, hid:]], axis=-1),
        ]
    )
    panels = to_tiles(panels.reshape(ncol, few, 2 * hid))
    rows = lax.dynamic_index_in_dim(blocks, lax.axis_index("zq"), 0, keepdims=False)
    rows = jnp.stack([rows[:, :, :hid], rows[:, :, hid:]])
    rows = to_tiles(jnp.pad(rows, ((0, 0), (0, 0), (0, 0), (0, LANES - hid))))
    n_panel, n_row = panels.shape[1], rows.shape[2]
    lead = (nx, npar, ncol)
    pieces = jnp.concatenate(
        [
            jnp.broadcast_to(panels, (nx, npar, *panels.shape)),
            jnp.broadcast_to(rows[:, :, None], (*lead, n_row, 8, 128)),
            jnp.broadcast_to(picked[:, :, None], (*lead, nz // 8, 8, 128)),
        ],
        axis=3,
    )
    pieces = exchange(pieces.reshape(nx * npar * ncol, -1, 8, 128), LEVELS)

    panel = from_tiles(pieces[:, :n_panel], few).reshape(-1, 2 * hid)
    row_block = from_tiles(pieces[:, n_panel : n_panel + n_row], few).reshape(-1, LANES)
    act_rows = pieces[:, n_panel + n_row :].reshape(nx, npar, ncol * nz, rfeat // 2)
    grad_cov, act_cov = covariances(row_block, panel, act_rows, cols, hid, 1.0 / token_count)
    return act_cov, grad_cov


def solution(mesh):
    fine = Mesh(mesh.devices.reshape(SIZES), AXES)
    placed = (P(ROW, None), P(COL, ROW), P(COL, ROW))
    return jax.shard_map(
        shards,
        mesh=fine,
        in_specs=placed,
        out_specs=(P(ROW, COL), P(ROW, COL)),
        check_vma=False,
    )
```
